32 devices in a mesh: seq: 8 (over z, y), chan: 4 (over x, core).
Axes of the slice: x: 2, y: 2, z: 4, core: 2. Of those that a mesh axis runs over, the one named last changes fastest.
Arguments:
- inputs: bfloat16 [1024, 4096], P('seq', 'chan'), may hold values from -6 to 6
- grads: bfloat16 [1024, 4096], P('seq', 'chan'), may hold values from -0.5 to 0.5
- filter_taps: float32 [256, 4096], P(('seq', 'chan')), may hold values from -6 to 6
- supports: int32 [32], replicated, may hold values from 1 to 2, as said below
Outputs:
- grad_inputs: bfloat16 [1024, 4096], P('seq', 'chan')
- grad_filter: float32 [256, 4096], P(('seq', 'chan'))
The draws below stay inside these ranges and needn't reach their ends.
Inputs may be any that keep to these rules, and one draw needn't show every extreme that they name: `supports`: some group spans 2 blocks and some group spans 1 block.
All inputs are finite; a program needn't handle non-finite values.
Results may differ from the reference program's by a relative error of at most 0.001.
Values may be sent and summed in bfloat16 or wider, within the bound.
No kernel may reach another device: no remote copies, remote signals or barrier semaphores. Data moves between devices by JAX's collectives and lax.ppermute only.
A program may use at most 64 MiB of HBM per device.

```python
import jax
import jax.numpy as jnp

TB = 128
GROUP_CH = 128
GROUPS = 32
CHANNELS = 4096
SEQ = 1024
SMAX = 2
LAGS = 256


def draw_supports(key, part):
    key = jax.random.fold_in(key, 1)
    values = jax.random.randint(jax.random.fold_in(key, 2), (GROUPS,), 1, SMAX + 1).astype(jnp.int32)
    order = jax.random.permutation(jax.random.fold_in(key, 3), GROUPS)
    values = values.at[order[0]].set(SMAX)
    values = values.at[order[1]].set(1)
    return values.astype(jnp.int32)


def block_scale(key, dims, cuts, least, largest):
    factor_of, own = 1.0, jax.random.fold_in(key, 6)
    for axis_at, shards_of in cuts:
        steps = jnp.exp(jax.random.uniform(jax.random.fold_in(own, axis_at), (shards_of,), jnp.float32, least / len(cuts), largest / len(cuts)))
        factor_of = factor_of * jnp.repeat(steps, dims[axis_at] // shards_of).reshape([-1 if axis == axis_at else 1 for axis in range(len(dims))])
    return factor_of


def normal_values(own_key, shape, deviation, bound, split=(), kind=jnp.bfloat16):
    gain = block_scale(own_key, shape, split, -0.22, 0.18) if split else 1.0
    entries = jax.random.normal(own_key, shape, jnp.float32) * deviation * gain
    return jnp.minimum(jnp.maximum(entries, -bound), bound).astype(kind)


def setup_inputs(seed: int = 0) -> dict:
    splits = jax.random.split(jax.random.key(seed), 5)
    inputs = normal_values(splits[0], (SEQ, CHANNELS), 1.0, 6.0, ((0, 8), (1, 4)))
    grads = normal_values(splits[1], (SEQ, CHANNELS), (SEQ ** -0.5), 0.5, ((0, 8), (1, 4)))
    filter_taps = normal_values(splits[2], (LAGS, CHANNELS), 1.0, 6.0, ((0, 32),), jnp.float32)
    supports = draw_supports(jax.random.fold_in(splits[4], 71), 0)
    return {"inputs": inputs, "grads": grads, "filter_taps": filter_taps, "supports": supports}


def reference(inputs, grads, filter_taps, supports):
    limit = jnp.repeat(supports, GROUP_CH) * TB
    lag_pos = jnp.arange(LAGS, dtype=jnp.int32)[:, None]
    taps = jnp.where(lag_pos < limit[None, :], filter_taps, jnp.zeros_like(filter_taps))
    signal = inputs.astype(jnp.float32)
    upstream = grads.astype(jnp.float32)
    span_len = 2 * SEQ
    grad_spec = jnp.fft.rfft(upstream, n=span_len, axis=0)
    tap_spec = jnp.fft.rfft(taps, n=span_len, axis=0)
    signal_spec = jnp.fft.rfft(signal, n=span_len, axis=0)
    grad_inputs = jnp.fft.irfft(grad_spec * jnp.conj(tap_spec), n=span_len, axis=0)[:SEQ]
    corr = jnp.fft.irfft(grad_spec * jnp.conj(signal_spec), n=span_len, axis=0)[:LAGS]
    grad_filter = jnp.where(lag_pos < limit[None, :], corr, jnp.zeros_like(corr))
    return grad_inputs.astype(jnp.bfloat16), grad_filter.astype(jnp.float32)
```

```python
import functools

import numpy as np
import ml_dtypes
import jax
import jax.numpy as jnp
from jax import lax
from jax.experimental import pallas as pl
from jax.experimental.pallas import tpu as pltpu
from jax.sharding import PartitionSpec as P

GROUP_CH = 128
LANES = 128
BF16 = jnp.bfloat16
F32 = jnp.float32
EVERY = ("seq", "chan")
VMEM = pl.BlockSpec(memory_space=pltpu.VMEM)
HBM = pl.BlockSpec(memory_space=pltpu.HBM)
SMEM = pl.BlockSpec(memory_space=pltpu.SMEM)
PARAMS = pltpu.CompilerParams(vmem_limit_bytes=40 * 1024 * 1024)


def split_table(table):
    high = table.astype(ml_dtypes.bfloat16)
    low = (table - high.astype(np.float64)).astype(ml_dtypes.bfloat16)
    return high, low


def tables(lags):
    freqs = np.concatenate([np.arange(0, lags, 2), np.arange(1, lags, 2)]) + 0.5
    angle = freqs[:, None] * np.arange(lags)[None, :] * (np.pi / lags)
    forward = np.concatenate([np.cos(angle), -np.sin(angle)], axis=0)
    parts = split_table(forward) + split_table(forward.T / lags)
    return [jnp.asarray(part) for part in parts]


def split_values(values):
    high = values.astype(BF16)
    return high, (values - high.astype(F32)).astype(BF16)


def split_outside(values):
    high = lax.reduce_precision(values, 8, 7)
    return [high.astype(BF16), (values - high).astype(BF16)]


def dot(first, second):
    return jnp.dot(first, second, preferred_element_type=F32)


def dot_exact(table, values):
    return dot(table[0], values) + dot(table[1], values)


def dot_split(table, values):
    high, low = split_values(values)
    return dot(table[0], high) + (dot(table[0], low) + dot(table[1], high))


def conj_product(first, second, half):
    first_re, first_im = first[:half], first[half:]
    second_re, second_im = second[:half], second[half:]
    return jnp.concatenate(
        [first_re * second_re + first_im * second_im, first_im * second_re - first_re * second_im], axis=0
    )


def add_next(own, following, lags):
    quarter = lags // 2
    parts = [own[i * quarter : (i + 1) * quarter] for i in range(4)]
    nexts = [following[i * quarter : (i + 1) * quarter] for i in range(4)]
    return jnp.concatenate(
        [parts[0] + nexts[2], parts[1] - nexts[3], parts[2] - nexts[0], parts[3] + nexts[1]], axis=0
    )


def conv_grads(lags, upstream, signal, taps, limit, forward, inverse):
    blocks, width = len(upstream), upstream[0].shape[1]
    if width == LANES:
        joined = dot_exact(forward, jnp.concatenate(upstream + signal + taps, axis=1))
        specs = [joined[:, k * width : (k + 1) * width] for k in range(2 * blocks + 2)]
    else:
        specs = [dot_exact(forward, part) for part in upstream + signal + taps]
    taps_spec = specs[2 * blocks] + specs[2 * blocks + 1]
    products, filter_spec = [], None
    for k in range(blocks):
        window = add_next(specs[k], specs[k + 1], lags) if k + 1 < blocks else specs[k]
        products.append(conj_product(window, taps_spec, lags))
        term = conj_product(window, specs[blocks + k], lags)
        filter_spec = term if filter_spec is None else filter_spec + term
    products.append(filter_spec)
    if width == LANES:
        joined = dot_split(inverse, jnp.concatenate(products, axis=1))
        results = [joined[:, k * width : (k + 1) * width] for k in range(blocks + 1)]
    else:
        results = [dot_split(inverse, product) for product in products]
    lag_pos = lax.broadcasted_iota(jnp.int32, results[-1].shape, 0)
    return results[:-1], jnp.where(lag_pos < limit, results[-1], 0.0)


def swap_table():
    quarter = LANES // 4
    index = np.arange(4 * LANES)
    part, block, lane = index // LANES, index % LANES // quarter, index % quarter
    target = block * LANES + part * quarter + lane
    table = np.zeros((4 * LANES, 4 * LANES), ml_dtypes.bfloat16)
    table[index, target] = 1
    return jnp.asarray(table)


def swap_blocks(stacks, table):
    rows = stacks[0][0].shape[0]
    side = [jnp.concatenate(parts, axis=1) for parts in stacks]
    moved = dot(jnp.concatenate(side, axis=0), table).astype(BF16)
    return [
        [moved[i * rows : (i + 1) * rows, l * LANES : (l + 1) * LANES] for l in range(4)] for i in range(len(stacks))
    ]


def split_rows(values):
    high = values.astype(BF16).astype(F32)
    return jnp.concatenate([high, values - high], axis=0).astype(BF16)


def pack_kernel(grad_hbm, signal_hbm, taps_hbm, table_hbm, out_ref, grad_ref, signal_ref, taps_ref, table_ref, sems):
    pairs = ((table_hbm, table_ref), (grad_hbm, grad_ref), (signal_hbm, signal_ref), (taps_hbm, taps_ref))
    copies = [pltpu.make_async_copy(source, target, sems.at[i]) for i, (source, target) in enumerate(pairs)]
    for copy in copies:
        copy.start()
    rows, width_here = grad_ref.shape
    piece = rows // 4
    tiles = range(width_here // LANES)
    copies[0].wait()
    table = table_ref[...]
    for at, source, copy in ((0, grad_ref, copies[1]), (piece, signal_ref, copies[2])):
        copy.wait()
        moved = swap_blocks(
            [
                [source[q * piece : (q + 1) * piece, tile * LANES : (tile + 1) * LANES] for q in range(4)]
                for tile in tiles
            ],
            table,
        )
        for tile in tiles:
            for l in range(4):
                out_ref[tile * 4 + l, at : at + piece, :] = moved[tile][l]
    copies[3].wait()
    starts = [[c * width_here + tile * LANES for c in range(4)] for tile in tiles]
    moved = swap_blocks([[split_rows(taps_ref[:, at : at + LANES]) for at in row] for row in starts], table)
    for tile in tiles:
        for l in range(4):
            out_ref[tile * 4 + l, 2 * piece :, :] = moved[tile][l]


def lane_limit(support_ref, width):
    lane = lax.broadcasted_iota(jnp.int32, (1, width), 1)
    parts = support_ref.shape[0]
    limit = jnp.zeros((1, width), jnp.int32)
    for part in range(parts):
        limit = jnp.where(lane >= part * (width // parts), support_ref[part] * GROUP_CH, limit)
    return limit


def mask_taps(parts, limit):
    lag_pos = lax.broadcasted_iota(jnp.int32, parts[0].shape, 0)
    return [jnp.where(lag_pos < limit, part, 0.0).astype(BF16) for part in parts]


def fast_kernel(lags, piece, support_ref, mixed_ref, table_ref, fwd_hi, fwd_lo, inv_hi, inv_lo, out_ref):
    devices, rows, width = mixed_ref.shape
    seq_count = devices // 4
    own = (rows - 2 * piece) // 2
    per_block = lags // (4 * piece)
    limit = lane_limit(support_ref, width)
    table = table_ref[...]

    def gathered(at):
        moved = swap_blocks(
            [[mixed_ref[s * 4 + c, at : at + piece, :] for c in range(4)] for s in range(seq_count)], table
        )
        flat = [part for parts in moved for part in parts]
        size = 4 * per_block
        return [jnp.concatenate(flat[k : k + size], axis=0) for k in range(0, len(flat), size)]

    tap_parts = mixed_ref[:, 2 * piece :, :].astype(F32)
    taps = mask_taps([tap_parts[:, i * own : (i + 1) * own].reshape(lags, width) for i in range(2)], limit)
    results, filter_grad = conv_grads(
        lags, gathered(0), gathered(piece), taps, limit, (fwd_hi[...], fwd_lo[...]), (inv_hi[...], inv_lo[...])
    )
    for j in range(devices):
        out_ref[j, piece:, :] = split_rows(filter_grad[j * own : (j + 1) * own])
    stacks = []
    for s in range(seq_count):
        result = results[s // per_block].astype(BF16)
        start = (s % per_block) * 4 * piece
        stacks.append([result[start + q * piece : start + (q + 1) * piece] for q in range(4)])
    moved = swap_blocks(stacks, table)
    for s in range(seq_count):
        for c in range(4):
            out_ref[s * 4 + c, 0:piece, :] = moved[s][c]


def unpack_kernel(mixed_ref, table_ref, out_hbm, filter_hbm, out_ref, filter_ref, sems):
    rows, width_here = out_ref.shape
    piece = rows // 4
    own = filter_ref.shape[0]
    tiles = range(width_here // LANES)
    table = table_ref[...]
    moved = swap_blocks([[mixed_ref[tile * 4 + l, 0:piece, :] for l in range(4)] for tile in tiles], table)
    for tile in tiles:
        for q in range(4):
            out_ref[q * piece : (q + 1) * piece, tile * LANES : (tile + 1) * LANES] = moved[tile][q]
    first = pltpu.make_async_copy(out_ref, out_hbm, sems.at[0])
    first.start()
    moved = swap_blocks([[mixed_ref[tile * 4 + l, piece:, :] for l in range(4)] for tile in tiles], table)
    for tile in tiles:
        for c in range(4):
            both = moved[tile][c].astype(F32)
            start = c * width_here + tile * LANES
            filter_ref[:, start : start + LANES] = both[:own] + both[own:]
    second = pltpu.make_async_copy(filter_ref, filter_hbm, sems.at[1])
    second.start()
    first.wait()
    second.wait()


def fast_body(inputs, grads, filter_taps, supports, seq_count, chan_count):
    block_len, width_here = inputs.shape
    rows_each = filter_taps.shape[0]
    devices = seq_count * chan_count
    lags = rows_each * devices
    piece = block_len // 4
    table = swap_table()
    groups_here = width_here // GROUP_CH
    own_support = lax.dynamic_slice_in_dim(
        supports.reshape(chan_count, groups_here), lax.axis_index("seq"), 1, 1
    ).reshape(chan_count)
    mixed = pl.pallas_call(
        pack_kernel,
        out_shape=jax.ShapeDtypeStruct((devices, 2 * piece + 2 * rows_each, LANES), BF16),
        in_specs=[HBM] * 4, out_specs=VMEM,
        scratch_shapes=[
            pltpu.VMEM(inputs.shape, BF16), pltpu.VMEM(inputs.shape, BF16),
            pltpu.VMEM(filter_taps.shape, F32), pltpu.VMEM(table.shape, BF16),
            pltpu.SemaphoreType.DMA((4,)),
        ],
        compiler_params=PARAMS, name="pack",
    )(grads, inputs, filter_taps, table)
    mixed = lax.all_to_all(mixed, EVERY, split_axis=0, concat_axis=0, tiled=True)
    mixed = pl.pallas_call(
        functools.partial(fast_kernel, lags, piece),
        out_shape=jax.ShapeDtypeStruct((devices, piece + 2 * rows_each, LANES), BF16),
        in_specs=[SMEM] + [VMEM] * 6, out_specs=VMEM, compiler_params=PARAMS, name="conv_grads",
    )(own_support, mixed, table, *tables(lags))
    mixed = lax.all_to_all(mixed, EVERY, split_axis=0, concat_axis=0, tiled=True)
    return pl.pallas_call(
        unpack_kernel,
        out_shape=(
            jax.ShapeDtypeStruct((block_len, width_here), BF16),
            jax.ShapeDtypeStruct(filter_taps.shape, F32),
        ),
        in_specs=[VMEM] * 2, out_specs=(HBM, HBM),
        scratch_shapes=[
            pltpu.VMEM((block_len, width_here), BF16), pltpu.VMEM(filter_taps.shape, F32),
            pltpu.SemaphoreType.DMA((2,)),
        ],
        compiler_params=PARAMS, name="unpack",
    )(mixed, table)


def plain_kernel(
    lags, support_ref, grad_ref, signal_ref, high_ref, low_ref, fwd_hi, fwd_lo, inv_hi, inv_lo, out_ref, filter_ref
):
    total, width = grad_ref.shape
    limit = lane_limit(support_ref, width)
    taps = mask_taps([high_ref[...].astype(F32), low_ref[...].astype(F32)], limit)
    cuts = [slice(k * lags, (k + 1) * lags) for k in range(total // lags)]
    results, filter_grad = conv_grads(
        lags, [grad_ref[cut, :] for cut in cuts], [signal_ref[cut, :] for cut in cuts], taps, limit,
        (fwd_hi[...], fwd_lo[...]), (inv_hi[...], inv_lo[...]),
    )
    for cut, result in zip(cuts, results):
        out_ref[cut, :] = result.astype(BF16)
    filter_ref[...] = filter_grad


def plain_body(inputs, grads, filter_taps, supports, seq_count, chan_count):
    block_len, width_here = inputs.shape
    rows_each = filter_taps.shape[0]
    devices = seq_count * chan_count
    lags = rows_each * devices
    total = block_len * seq_count
    share = width_here // devices
    width = share * chan_count
    index = lax.axis_index("seq") * chan_count + lax.axis_index("chan")
    groups_here = width_here // GROUP_CH
    own_support = lax.dynamic_slice_in_dim(
        supports.reshape(chan_count, groups_here), index * share // GROUP_CH, 1, 1
    ).reshape(chan_count)

    def sent(values):
        return values.reshape(block_len, devices, share).transpose(1, 0, 2).reshape(devices, -1)

    def received(values):
        return values.reshape(seq_count, chan_count, block_len, share).transpose(0, 2, 1, 3).reshape(total, width)

    taps = filter_taps.reshape(rows_each, chan_count, devices, share).transpose(2, 0, 1, 3).reshape(devices, -1)
    mixed = jnp.concatenate([sent(grads), sent(inputs), *split_outside(taps)], axis=1)
    mixed = lax.all_to_all(mixed, EVERY, split_axis=0, concat_axis=0, tiled=True)
    part, own = block_len * share, rows_each * width
    upstream, signal = received(mixed[:, :part]), received(mixed[:, part : 2 * part])
    taps_high = mixed[:, 2 * part : 2 * part + own].reshape(lags, width)
    taps_low = mixed[:, 2 * part + own :].reshape(lags, width)
    result, filter_grad = pl.pallas_call(
        functools.partial(plain_kernel, lags),
        out_shape=(jax.ShapeDtypeStruct((total, width), BF16), jax.ShapeDtypeStruct((lags, width), F32)),
        in_specs=[SMEM] + [VMEM] * 8, out_specs=(VMEM, VMEM), compiler_params=PARAMS, name="conv_grads",
    )(own_support, upstream, signal, taps_high, taps_low, *tables(lags))
    result = result.reshape(seq_count, block_len, chan_count, share).transpose(0, 2, 1, 3).reshape(devices, part)
    mixed = jnp.concatenate([result, *split_outside(filter_grad.reshape(devices, own))], axis=1)
    mixed = lax.all_to_all(mixed, EVERY, split_axis=0, concat_axis=0, tiled=True)
    grad_inputs = mixed[:, :part].reshape(devices, block_len, share).transpose(1, 0, 2).reshape(block_len, width_here)
    filter_grad = mixed[:, part : part + own].astype(F32) + mixed[:, part + own :].astype(F32)
    filter_grad = filter_grad.reshape(devices, rows_each, chan_count, share).transpose(1, 2, 0, 3)
    return grad_inputs, filter_grad.reshape(filter_taps.shape)


def solution(mesh):
    seq_count, chan_count = mesh.shape["seq"], mesh.shape["chan"]

    def body(inputs, grads, filter_taps, supports):
        share = inputs.shape[1] // (seq_count * chan_count)
        lags = filter_taps.shape[0] * seq_count * chan_count
        fits = chan_count == 4 and share * 4 == LANES and filter_taps.shape[0] % 8 == 0
        fits = fits and inputs.shape[0] % 64 == 0 and lags % inputs.shape[0] == 0
        chosen = fast_body if fits else plain_body
        return chosen(inputs, grads, filter_taps, supports, seq_count, chan_count)

    in_specs = (P("seq", "chan"), P("seq", "chan"), P(("seq", "chan"), None), P())
    out_specs = (P("seq", "chan"), P(("seq", "chan"), None))
    return jax.shard_map(body, mesh=mesh, in_specs=in_specs, out_specs=out_specs, check_vma=False)
```

```python
import functools

import numpy as np
import ml_dtypes
import jax
import jax.numpy as jnp
from jax import lax
from jax.experimental import pallas as pl
from jax.experimental.pallas import tpu as pltpu
from jax.sharding import PartitionSpec as P

GROUP_CH = 128
LANES = 128
BF16 = jnp.bfloat16
F32 = jnp.float32
EVERY = ("seq", "chan")
VMEM = pl.BlockSpec(memory_space=pltpu.VMEM)
HBM = pl.BlockSpec(memory_space=pltpu.HBM)
SMEM = pl.BlockSpec(memory_space=pltpu.SMEM)
PARAMS = pltpu.CompilerParams(vmem_limit_bytes=40 * 1024 * 1024)


def split_table(table):
    high = table.astype(ml_dtypes.bfloat16)
    low = (table - high.astype(np.float64)).astype(ml_dtypes.bfloat16)
    return high, low


def tables(lags):
    freqs = np.concatenate([np.arange(0, lags, 2), np.arange(1, lags, 2)]) + 0.5
    angle = freqs[:, None] * np.arange(lags)[None, :] * (np.pi / lags)
    forward = np.concatenate([np.cos(angle), -np.sin(angle)], axis=0)
    high, low = split_table(forward)
    back_high, back_low = split_table(forward.T / lags)
    joined = (np.concatenate([high, low], axis=1), np.concatenate([back_high, back_high, back_low], axis=1))
    return [jnp.asarray(part) for part in joined]


def split_values(values):
    high = values.astype(BF16)
    return high, (values - high.astype(F32)).astype(BF16)


def split_outside(values):
    high = lax.reduce_precision(values, 8, 7)
    return [high.astype(BF16), (values - high).astype(BF16)]


def dot(first, second):
    return jnp.dot(first, second, preferred_element_type=F32)


def dot_exact(table, values):
    return dot(table, jnp.concatenate([values, values], axis=0))


def dot_split(table, values):
    high, low = split_values(values)
    return dot(table, jnp.concatenate([high, low, high], axis=0))


def conj_product(first, second, half):
    first_re, first_im = first[:half], first[half:]
    second_re, second_im = second[:half], second[half:]
    return jnp.concatenate(
        [first_re * second_re + first_im * second_im, first_im * second_re - first_re * second_im], axis=0
    )


def add_next(own, following, lags):
    quarter = lags // 2
    parts = [own[i * quarter : (i + 1) * quarter] for i in range(4)]
    nexts = [following[i * quarter : (i + 1) * quarter] for i in range(4)]
    return jnp.concatenate(
        [parts[0] + nexts[2], parts[1] - nexts[3], parts[2] - nexts[0], parts[3] + nexts[1]], axis=0
    )


def conv_grads(lags, upstream, signal, taps, limit, forward, inverse):
    blocks, width = len(upstream), upstream[0].shape[1]
    if width == LANES:
        joined = dot_exact(forward, jnp.concatenate(upstream + signal + taps, axis=1))
        specs = [joined[:, k * width : (k + 1) * width] for k in range(2 * blocks + 2)]
    else:
        specs = [dot_exact(forward, part) for part in upstream + signal + taps]
    taps_spec = specs[2 * blocks] + specs[2 * blocks + 1]
    products, filter_spec = [], None
    for k in range(blocks):
        window = add_next(specs[k], specs[k + 1], lags) if k + 1 < blocks else specs[k]
        products.append(conj_product(window, taps_spec, lags))
        term = conj_product(window, specs[blocks + k], lags)
        filter_spec = term if filter_spec is None else filter_spec + term
    products.append(filter_spec)
    if width == LANES:
        joined = dot_split(inverse, jnp.concatenate(products, axis=1))
        results = [joined[:, k * width : (k + 1) * width] for k in range(blocks + 1)]
    else:
        results = [dot_split(inverse, product) for product in products]
    lag_pos = lax.broadcasted_iota(jnp.int32, results[-1].shape, 0)
    return results[:-1], jnp.where(lag_pos < limit, results[-1], 0.0)


def swap_table():
    quarter = LANES // 4
    index = np.arange(4 * LANES)
    part, block, lane = index // LANES, index % LANES // quarter, index % quarter
    target = block * LANES + part * quarter + lane
    table = np.zeros((4 * LANES, 4 * LANES), ml_dtypes.bfloat16)
    table[index, target] = 1
    return jnp.asarray(table)


def swap_blocks(stacks, table):
    rows = stacks[0][0].shape[0]
    side = [jnp.concatenate(parts, axis=1) for parts in stacks]
    moved = dot(jnp.concatenate(side, axis=0), table).astype(BF16)
    return [
        [moved[i * rows : (i + 1) * rows, l * LANES : (l + 1) * LANES] for l in range(4)] for i in range(len(stacks))
    ]


def split_rows(values):
    high = values.astype(BF16).astype(F32)
    return jnp.concatenate([high, values - high], axis=0).astype(BF16)


def pack_kernel(
    grad_hbm, signal_hbm, taps_hbm, table_hbm, out_hbm, grad_ref, signal_ref, taps_ref, table_ref, out_ref, sems
):
    pairs = ((table_hbm, table_ref), (grad_hbm, grad_ref), (signal_hbm, signal_ref), (taps_hbm, taps_ref))
    arriving = [pltpu.make_async_copy(source, target, sems.at[i]) for i, (source, target) in enumerate(pairs)]
    for copy in arriving:
        copy.start()
    rows, width_here = grad_ref.shape
    piece = rows // 4
    tiles = range(width_here // LANES)
    cuts = [slice(0, piece), slice(piece, 2 * piece), slice(2 * piece, out_ref.shape[1])]
    leaving = [
        pltpu.make_async_copy(out_ref.at[:, cut, :], out_hbm.at[:, cut, :], sems.at[4 + i])
        for i, cut in enumerate(cuts)
    ]

    def moved_out(index, stacks):
        moved = swap_blocks(stacks, table)
        for tile in tiles:
            for l in range(4):
                out_ref[tile * 4 + l, cuts[index], :] = moved[tile][l]
        leaving[index].start()

    arriving[0].wait()
    table = table_ref[...]
    for index, source in enumerate((grad_ref, signal_ref)):
        arriving[1 + index].wait()
        moved_out(
            index,
            [
                [source[q * piece : (q + 1) * piece, tile * LANES : (tile + 1) * LANES] for q in range(4)]
                for tile in tiles
            ],
        )
    arriving[3].wait()
    starts = [[c * width_here + tile * LANES for c in range(4)] for tile in tiles]
    moved_out(2, [[split_rows(taps_ref[:, at : at + LANES]) for at in row] for row in starts])
    for copy in leaving:
        copy.wait()


def lane_limit(support_ref, width):
    lane = lax.broadcasted_iota(jnp.int32, (1, width), 1)
    parts = support_ref.shape[0]
    limit = jnp.zeros((1, width), jnp.int32)
    for part in range(parts):
        limit = jnp.where(lane >= part * (width // parts), support_ref[part] * GROUP_CH, limit)
    return limit


def mask_taps(parts, limit):
    lag_pos = lax.broadcasted_iota(jnp.int32, parts[0].shape, 0)
    return [jnp.where(lag_pos < limit, part, 0.0).astype(BF16) for part in parts]


def fast_kernel(lags, piece, support_ref, mixed_ref, table_ref, forward_ref, inverse_ref, out_ref):
    devices, rows, width = mixed_ref.shape
    seq_count = devices // 4
    own = (rows - 2 * piece) // 2
    per_block = lags // (4 * piece)
    limit = lane_limit(support_ref, width)
    table = table_ref[...]

    def gathered(at):
        moved = swap_blocks(
            [[mixed_ref[s * 4 + c, at : at + piece, :] for c in range(4)] for s in range(seq_count)], table
        )
        flat = [part for parts in moved for part in parts]
        size = 4 * per_block
        return [jnp.concatenate(flat[k : k + size], axis=0) for k in range(0, len(flat), size)]

    tap_parts = mixed_ref[:, 2 * piece :, :].astype(F32)
    taps = mask_taps([tap_parts[:, i * own : (i + 1) * own].reshape(lags, width) for i in range(2)], limit)
    results, filter_grad = conv_grads(
        lags, gathered(0), gathered(piece), taps, limit, forward_ref[...], inverse_ref[...]
    )
    for j in range(devices):
        out_ref[j, piece:, :] = split_rows(filter_grad[j * own : (j + 1) * own])
    stacks = []
    for s in range(seq_count):
        result = results[s // per_block].astype(BF16)
        start = (s % per_block) * 4 * piece
        stacks.append([result[start + q * piece : start + (q + 1) * piece] for q in range(4)])
    moved = swap_blocks(stacks, table)
    for s in range(seq_count):
        for c in range(4):
            out_ref[s * 4 + c, 0:piece, :] = moved[s][c]


def unpack_kernel(mixed_ref, table_ref, out_hbm, filter_hbm, out_ref, filter_ref, sems):
    rows, width_here = out_ref.shape
    piece = rows // 4
    own = filter_ref.shape[0]
    tiles = range(width_here // LANES)
    table = table_ref[...]
    moved = swap_blocks([[mixed_ref[tile * 4 + l, 0:piece, :] for l in range(4)] for tile in tiles], table)
    for tile in tiles:
        for q in range(4):
            out_ref[q * piece : (q + 1) * piece, tile * LANES : (tile + 1) * LANES] = moved[tile][q]
    first = pltpu.make_async_copy(out_ref, out_hbm, sems.at[0])
    first.start()
    moved = swap_blocks([[mixed_ref[tile * 4 + l, piece:, :] for l in range(4)] for tile in tiles], table)
    for tile in tiles:
        for c in range(4):
            both = moved[tile][c].astype(F32)
            start = c * width_here + tile * LANES
            filter_ref[:, start : start + LANES] = both[:own] + both[own:]
    second = pltpu.make_async_copy(filter_ref, filter_hbm, sems.at[1])
    second.start()
    first.wait()
    second.wait()


def fast_body(inputs, grads, filter_taps, supports, seq_count, chan_count):
    block_len, width_here = inputs.shape
    rows_each = filter_taps.shape[0]
    devices = seq_count * chan_count
    lags = rows_each * devices
    piece = block_len // 4
    table = swap_table()
    groups_here = width_here // GROUP_CH
    own_support = lax.dynamic_slice_in_dim(
        supports.reshape(chan_count, groups_here), lax.axis_index("seq"), 1, 1
    ).reshape(chan_count)
    mixed = pl.pallas_call(
        pack_kernel,
        out_shape=jax.ShapeDtypeStruct((devices, 2 * piece + 2 * rows_each, LANES), BF16),
        in_specs=[HBM] * 4, out_specs=HBM,
        scratch_shapes=[
            pltpu.VMEM(inputs.shape, BF16), pltpu.VMEM(inputs.shape, BF16),
            pltpu.VMEM(filter_taps.shape, F32), pltpu.VMEM(table.shape, BF16),
            pltpu.VMEM((devices, 2 * piece + 2 * rows_each, LANES), BF16),
            pltpu.SemaphoreType.DMA((7,)),
        ],
        compiler_params=pltpu.CompilerParams(vmem_limit_bytes=60 * 1024 * 1024), name="pack",
    )(grads, inputs, filter_taps, table)
    mixed = lax.all_to_all(mixed, EVERY, split_axis=0, concat_axis=0, tiled=True)
    mixed = pl.pallas_call(
        functools.partial(fast_kernel, lags, piece),
        out_shape=jax.ShapeDtypeStruct((devices, piece + 2 * rows_each, LANES), BF16),
        in_specs=[SMEM] + [VMEM] * 4, out_specs=VMEM, compiler_params=PARAMS, name="conv_grads",
    )(own_support, mixed, table, *tables(lags))
    mixed = lax.all_to_all(mixed, EVERY, split_axis=0, concat_axis=0, tiled=True)
    return pl.pallas_call(
        unpack_kernel,
        out_shape=(
            jax.ShapeDtypeStruct((block_len, width_here), BF16),
            jax.ShapeDtypeStruct(filter_taps.shape, F32),
        ),
        in_specs=[VMEM] * 2, out_specs=(HBM, HBM),
        scratch_shapes=[
            pltpu.VMEM((block_len, width_here), BF16), pltpu.VMEM(filter_taps.shape, F32),
            pltpu.SemaphoreType.DMA((2,)),
        ],
        compiler_params=PARAMS, name="unpack",
    )(mixed, table)


def plain_kernel(
    lags, support_ref, grad_ref, signal_ref, high_ref, low_ref, forward_ref, inverse_ref, out_ref, filter_ref
):
    total, width = grad_ref.shape
    limit = lane_limit(support_ref, width)
    taps = mask_taps([high_ref[...].astype(F32), low_ref[...].astype(F32)], limit)
    cuts = [slice(k * lags, (k + 1) * lags) for k in range(total // lags)]
    results, filter_grad = conv_grads(
        lags, [grad_ref[cut, :] for cut in cuts], [signal_ref[cut, :] for cut in cuts], taps, limit,
        forward_ref[...], inverse_ref[...],
    )
    for cut, result in zip(cuts, results):
        out_ref[cut, :] = result.astype(BF16)
    filter_ref[...] = filter_grad


def plain_body(inputs, grads, filter_taps, supports, seq_count, chan_count):
    block_len, width_here = inputs.shape
    rows_each = filter_taps.shape[0]
    devices = seq_count * chan_count
    lags = rows_each * devices
    total = block_len * seq_count
    share = width_here // devices
    width = share * chan_count
    index = lax.axis_index("seq") * chan_count + lax.axis_index("chan")
    groups_here = width_here // GROUP_CH
    own_support = lax.dynamic_slice_in_dim(
        supports.reshape(chan_count, groups_here), index * share // GROUP_CH, 1, 1
    ).reshape(chan_count)

    def sent(values):
        return values.reshape(block_len, devices, share).transpose(1, 0, 2).reshape(devices, -1)

    def received(values):
        return values.reshape(seq_count, chan_count, block_len, share).transpose(0, 2, 1, 3).reshape(total, width)

    taps = filter_taps.reshape(rows_each, chan_count, devices, share).transpose(2, 0, 1, 3).reshape(devices, -1)
    mixed = jnp.concatenate([sent(grads), sent(inputs), *split_outside(taps)], axis=1)
    mixed = lax.all_to_all(mixed, EVERY, split_axis=0, concat_axis=0, tiled=True)
    part, own = block_len * share, rows_each * width
    upstream, signal = received(mixed[:, :part]), received(mixed[:, part : 2 * part])
    taps_high = mixed[:, 2 * part : 2 * part + own].reshape(lags, width)
    taps_low = mixed[:, 2 * part + own :].reshape(lags, width)
    result, filter_grad = pl.pallas_call(
        functools.partial(plain_kernel, lags),
        out_shape=(jax.ShapeDtypeStruct((total, width), BF16), jax.ShapeDtypeStruct((lags, width), F32)),
        in_specs=[SMEM] + [VMEM] * 6, out_specs=(VMEM, VMEM), compiler_params=PARAMS, name="conv_grads",
    )(own_support, upstream, signal, taps_high, taps_low, *tables(lags))
    result = result.reshape(seq_count, block_len, chan_count, share).transpose(0, 2, 1, 3).reshape(devices, part)
    mixed = jnp.concatenate([result, *split_outside(filter_grad.reshape(devices, own))], axis=1)
    mixed = lax.all_to_all(mixed, EVERY, split_axis=0, concat_axis=0, tiled=True)
    grad_inputs = mixed[:, :part].reshape(devices, block_len, share).transpose(1, 0, 2).reshape(block_len, width_here)
    filter_grad = mixed[:, part : part + own].astype(F32) + mixed[:, part + own :].astype(F32)
    filter_grad = filter_grad.reshape(devices, rows_each, chan_count, share).transpose(1, 2, 0, 3)
    return grad_inputs, filter_grad.reshape(filter_taps.shape)


def solution(mesh):
    seq_count, chan_count = mesh.shape["seq"], mesh.shape["chan"]

    def body(inputs, grads, filter_taps, supports):
        share = inputs.shape[1] // (seq_count * chan_count)
        lags = filter_taps.shape[0] * seq_count * chan_count
        fits = chan_count == 4 and share * 4 == LANES and filter_taps.shape[0] % 8 == 0
        fits = fits and inputs.shape[0] % 64 == 0 and lags % inputs.shape[0] == 0
        chosen = fast_body if fits else plain_body
        return chosen(inputs, grads, filter_taps, supports, seq_count, chan_count)

    in_specs = (P("seq", "chan"), P("seq", "chan"), P(("seq", "chan"), None), P())
    out_specs = (P("seq", "chan"), P(("seq", "chan"), None))
    return jax.shard_map(body, mesh=mesh, in_specs=in_specs, out_specs=out_specs, check_vma=False)
```

```python
import functools

import numpy as np
import ml_dtypes
import jax
import jax.numpy as jnp
from jax import lax
from jax.experimental import pallas as pl
from jax.experimental.pallas import tpu as pltpu
from jax.sharding import PartitionSpec as P

GROUP_CH = 128
LANES = 128
BF16 = jnp.bfloat16
F32 = jnp.float32
EVERY = ("seq", "chan")
VMEM = pl.BlockSpec(memory_space=pltpu.VMEM)
HBM = pl.BlockSpec(memory_space=pltpu.HBM)
SMEM = pl.BlockSpec(memory_space=pltpu.SMEM)
PARAMS = pltpu.CompilerParams(vmem_limit_bytes=40 * 1024 * 1024)


def split_table(table):
    high = table.astype(ml_dtypes.bfloat16)
    low = (table - high.astype(np.float64)).astype(ml_dtypes.bfloat16)
    return high, low


def tables(lags):
    freqs = np.concatenate([np.arange(0, lags, 2), np.arange(1, lags, 2)]) + 0.5
    angle = freqs[:, None] * np.arange(lags)[None, :] * (np.pi / lags)
    forward = np.concatenate([np.cos(angle), -np.sin(angle)], axis=0)
    high, low = split_table(forward)
    back_high, back_low = split_table(forward.T / lags)
    joined = (np.concatenate([high, low], axis=1), np.concatenate([back_high, back_high, back_low], axis=1))
    return [jnp.asarray(part) for part in joined]


def split_values(values):
    high = values.astype(BF16)
    return high, (values - high.astype(F32)).astype(BF16)


def split_outside(values):
    high = lax.reduce_precision(values, 8, 7)
    return [high.astype(BF16), (values - high).astype(BF16)]


def dot(first, second):
    return jnp.dot(first, second, preferred_element_type=F32)


def dot_exact(table, values):
    return dot(table, jnp.concatenate([values, values], axis=0))


def dot_split(table, values):
    high, low = split_values(values)
    return dot(table, jnp.concatenate([high, low, high], axis=0))


def conj_product(first, second, half):
    first_re, first_im = first[:half], first[half:]
    second_re, second_im = second[:half], second[half:]
    return jnp.concatenate(
        [first_re * second_re + first_im * second_im, first_im * second_re - first_re * second_im], axis=0
    )


def add_next(own, following, lags):
    quarter = lags // 2
    parts = [own[i * quarter : (i + 1) * quarter] for i in range(4)]
    nexts = [following[i * quarter : (i + 1) * quarter] for i in range(4)]
    return jnp.concatenate(
        [parts[0] + nexts[2], parts[1] - nexts[3], parts[2] - nexts[0], parts[3] + nexts[1]], axis=0
    )


def transform(dot_with, table, parts):
    width = parts[0].shape[1]
    group = 2 if width == LANES else 1
    found = []
    for i in range(0, len(parts), group):
        pair = parts[i : i + group]
        joined = dot_with(table, jnp.concatenate(pair, axis=1) if len(pair) > 1 else pair[0])
        found += [joined[:, k * width : (k + 1) * width] for k in range(len(pair))]
    return found


def conv_grads(lags, upstream, signal, taps, limit, forward, inverse):
    blocks = len(upstream)
    taps_high, taps_low = transform(dot_exact, forward, taps)
    taps_spec = taps_high + taps_low
    specs = transform(dot_exact, forward, upstream)
    results, filter_spec = [], None
    for start in range(0, blocks, 2):
        pair = range(start, min(start + 2, blocks))
        signal_specs = transform(dot_exact, forward, [signal[k] for k in pair])
        windows = [add_next(specs[k], specs[k + 1], lags) if k + 1 < blocks else specs[k] for k in pair]
        results += transform(dot_split, inverse, [conj_product(window, taps_spec, lags) for window in windows])
        for window, signal_spec in zip(windows, signal_specs):
            term = conj_product(window, signal_spec, lags)
            filter_spec = term if filter_spec is None else filter_spec + term
    (filter_grad,) = transform(dot_split, inverse, [filter_spec])
    lag_pos = lax.broadcasted_iota(jnp.int32, filter_grad.shape, 0)
    return results, jnp.where(lag_pos < limit, filter_grad, 0.0)


def swap_table():
    quarter = LANES // 4
    row = lax.broadcasted_iota(jnp.int32, (quarter, LANES), 0)
    lane = lax.broadcasted_iota(jnp.int32, (quarter, LANES), 1)
    zeros = jnp.zeros((quarter, LANES), BF16)
    slabs = []
    for part in range(4):
        pattern = jnp.where(lane == row + part * quarter, 1.0, 0.0).astype(BF16)
        slabs += [
            jnp.concatenate([pattern if at == block else zeros for at in range(4)], axis=1) for block in range(4)
        ]
    return jnp.concatenate(slabs, axis=0)


def swap_blocks(stacks, table):
    rows = stacks[0][0].shape[0]
    side = [jnp.concatenate(parts, axis=1) for parts in stacks]
    moved = dot(jnp.concatenate(side, axis=0), table).astype(BF16)
    return [
        [moved[i * rows : (i + 1) * rows, l * LANES : (l + 1) * LANES] for l in range(4)] for i in range(len(stacks))
    ]


def split_rows(values):
    high = values.astype(BF16).astype(F32)
    return jnp.concatenate([high, values - high], axis=0).astype(BF16)


def pack_kernel(grad_hbm, signal_hbm, taps_hbm, out_ref, grad_ref, signal_ref, taps_ref, sems):
    pairs = ((grad_hbm, grad_ref), (signal_hbm, signal_ref), (taps_hbm, taps_ref))
    arriving = [pltpu.make_async_copy(source, target, sems.at[i]) for i, (source, target) in enumerate(pairs)]
    for copy in arriving:
        copy.start()
    rows, width_here = grad_ref.shape
    piece = rows // 4
    tiles = range(width_here // LANES)

    def moved_out(cut, stacks):
        moved = swap_blocks(stacks, table)
        for tile in tiles:
            for l in range(4):
                out_ref[tile * 4 + l, cut, :] = moved[tile][l]

    table = swap_table()
    for index, source in enumerate((grad_ref, signal_ref)):
        arriving[index].wait()
        moved_out(
            slice(index * piece, (index + 1) * piece),
            [
                [source[q * piece : (q + 1) * piece, tile * LANES : (tile + 1) * LANES] for q in range(4)]
                for tile in tiles
            ],
        )
    arriving[2].wait()
    starts = [[c * width_here + tile * LANES for c in range(4)] for tile in tiles]
    moved_out(
        slice(2 * piece, out_ref.shape[1]),
        [[split_rows(taps_ref[:, at : at + LANES]) for at in row] for row in starts],
    )


def lane_limit(supports, width):
    lane = lax.broadcasted_iota(jnp.int32, (1, width), 1)
    limit = jnp.zeros((1, width), jnp.int32)
    for part, support in enumerate(supports):
        limit = jnp.where(lane >= part * (width // len(supports)), support * GROUP_CH, limit)
    return limit


def mask_taps(parts, limit):
    lag_pos = lax.broadcasted_iota(jnp.int32, parts[0].shape, 0)
    return [jnp.where(lag_pos < limit, part, 0.0).astype(BF16) for part in parts]


def fast_kernel(
    lags, piece, support_hbm, mixed_ref, forward_ref, inverse_ref, out_ref, support_ref, sem
):
    support_copy = pltpu.make_async_copy(support_hbm, support_ref, sem)
    support_copy.start()
    devices, rows, width = mixed_ref.shape
    seq_count = devices // 4
    own = (rows - 2 * piece) // 2
    per_block = lags // (4 * piece)
    table = swap_table()

    def gathered(at):
        moved = swap_blocks(
            [[mixed_ref[s * 4 + c, at : at + piece, :] for c in range(4)] for s in range(seq_count)], table
        )
        flat = [part for parts in moved for part in parts]
        size = 4 * per_block
        return [jnp.concatenate(flat[k : k + size], axis=0) for k in range(0, len(flat), size)]

    upstream, signal = gathered(0), gathered(piece)
    tap_parts = mixed_ref[:, 2 * piece :, :].astype(F32)
    groups_here = support_ref.shape[0] // 4
    index = lax.axis_index("seq")
    support_copy.wait()
    limit = lane_limit([support_ref[c * groups_here + index] for c in range(4)], width)
    taps = mask_taps([tap_parts[:, i * own : (i + 1) * own].reshape(lags, width) for i in range(2)], limit)
    results, filter_grad = conv_grads(lags, upstream, signal, taps, limit, forward_ref[...], inverse_ref[...])
    for j in range(devices):
        out_ref[j, piece:, :] = split_rows(filter_grad[j * own : (j + 1) * own])
    stacks = []
    for s in range(seq_count):
        result = results[s // per_block].astype(BF16)
        start = (s % per_block) * 4 * piece
        stacks.append([result[start + q * piece : start + (q + 1) * piece] for q in range(4)])
    moved = swap_blocks(stacks, table)
    for s in range(seq_count):
        for c in range(4):
            out_ref[s * 4 + c, 0:piece, :] = moved[s][c]


def unpack_kernel(mixed_ref, out_hbm, filter_hbm, out_ref, filter_ref, sems):
    rows, width_here = out_ref.shape
    piece = rows // 4
    own = filter_ref.shape[0]
    tiles = range(width_here // LANES)
    table = swap_table()
    moved = swap_blocks([[mixed_ref[tile * 4 + l, 0:piece, :] for l in range(4)] for tile in tiles], table)
    for tile in tiles:
        for q in range(4):
            out_ref[q * piece : (q + 1) * piece, tile * LANES : (tile + 1) * LANES] = moved[tile][q]
    first = pltpu.make_async_copy(out_ref, out_hbm, sems.at[0])
    first.start()
    moved = swap_blocks([[mixed_ref[tile * 4 + l, piece:, :] for l in range(4)] for tile in tiles], table)
    for tile in tiles:
        for c in range(4):
            both = moved[tile][c].astype(F32)
            start = c * width_here + tile * LANES
            filter_ref[:, start : start + LANES] = both[:own] + both[own:]
    second = pltpu.make_async_copy(filter_ref, filter_hbm, sems.at[1])
    second.start()
    first.wait()
    second.wait()


def fast_body(inputs, grads, filter_taps, supports, seq_count, chan_count):
    block_len, width_here = inputs.shape
    rows_each = filter_taps.shape[0]
    devices = seq_count * chan_count
    lags = rows_each * devices
    piece = block_len // 4
    sources = [pltpu.with_memory_space_constraint(part, pltpu.HBM) for part in (grads, inputs, filter_taps)]
    mixed = pl.pallas_call(
        pack_kernel,
        out_shape=pltpu.VMEM((devices, 2 * piece + 2 * rows_each, LANES), BF16),
        in_specs=[HBM] * 3, out_specs=VMEM,
        scratch_shapes=[
            pltpu.VMEM(inputs.shape, BF16), pltpu.VMEM(inputs.shape, BF16),
            pltpu.VMEM(filter_taps.shape, F32), pltpu.SemaphoreType.DMA((3,)),
        ],
        compiler_params=PARAMS, name="pack",
    )(*sources)
    mixed = lax.all_to_all(mixed, EVERY, split_axis=0, concat_axis=0, tiled=True)
    mixed = pl.pallas_call(
        functools.partial(fast_kernel, lags, piece),
        out_shape=jax.ShapeDtypeStruct((devices, piece + 2 * rows_each, LANES), BF16),
        in_specs=[HBM] + [VMEM] * 3, out_specs=VMEM,
        scratch_shapes=[pltpu.SMEM(supports.shape, jnp.int32), pltpu.SemaphoreType.DMA],
        compiler_params=PARAMS, name="conv_grads",
    )(pltpu.with_memory_space_constraint(supports, pltpu.HBM), mixed, *tables(lags))
    mixed = lax.all_to_all(mixed, EVERY, split_axis=0, concat_axis=0, tiled=True)
    return pl.pallas_call(
        unpack_kernel,
        out_shape=(
            jax.ShapeDtypeStruct((block_len, width_here), BF16),
            jax.ShapeDtypeStruct(filter_taps.shape, F32),
        ),
        in_specs=[VMEM], out_specs=(HBM, HBM),
        scratch_shapes=[
            pltpu.VMEM((block_len, width_here), BF16), pltpu.VMEM(filter_taps.shape, F32),
            pltpu.SemaphoreType.DMA((2,)),
        ],
        compiler_params=PARAMS, name="unpack",
    )(mixed)


def plain_kernel(
    lags, support_ref, grad_ref, signal_ref, high_ref, low_ref, forward_ref, inverse_ref, out_ref, filter_ref
):
    total, width = grad_ref.shape
    limit = lane_limit([support_ref[part] for part in range(support_ref.shape[0])], width)
    taps = mask_taps([high_ref[...].astype(F32), low_ref[...].astype(F32)], limit)
    cuts = [slice(k * lags, (k + 1) * lags) for k in range(total // lags)]
    results, filter_grad = conv_grads(
        lags, [grad_ref[cut, :] for cut in cuts], [signal_ref[cut, :] for cut in cuts], taps, limit,
        forward_ref[...], inverse_ref[...],
    )
    for cut, result in zip(cuts, results):
        out_ref[cut, :] = result.astype(BF16)
    filter_ref[...] = filter_grad


def plain_body(inputs, grads, filter_taps, supports, seq_count, chan_count):
    block_len, width_here = inputs.shape
    rows_each = filter_taps.shape[0]
    devices = seq_count * chan_count
    lags = rows_each * devices
    total = block_len * seq_count
    share = width_here // devices
    width = share * chan_count
    index = lax.axis_index("seq") * chan_count + lax.axis_index("chan")
    groups_here = width_here // GROUP_CH
    own_support = lax.dynamic_slice_in_dim(
        supports.reshape(chan_count, groups_here), index * share // GROUP_CH, 1, 1
    ).reshape(chan_count)

    def sent(values):
        return values.reshape(block_len, devices, share).transpose(1, 0, 2).reshape(devices, -1)

    def received(values):
        return values.reshape(seq_count, chan_count, block_len, share).transpose(0, 2, 1, 3).reshape(total, width)

    taps = filter_taps.reshape(rows_each, chan_count, devices, share).transpose(2, 0, 1, 3).reshape(devices, -1)
    mixed = jnp.concatenate([sent(grads), sent(inputs), *split_outside(taps)], axis=1)
    mixed = lax.all_to_all(mixed, EVERY, split_axis=0, concat_axis=0, tiled=True)
    part, own = block_len * share, rows_each * width
    upstream, signal = received(mixed[:, :part]), received(mixed[:, part : 2 * part])
    taps_high = mixed[:, 2 * part : 2 * part + own].reshape(lags, width)
    taps_low = mixed[:, 2 * part + own :].reshape(lags, width)
    result, filter_grad = pl.pallas_call(
        functools.partial(plain_kernel, lags),
        out_shape=(jax.ShapeDtypeStruct((total, width), BF16), jax.ShapeDtypeStruct((lags, width), F32)),
        in_specs=[SMEM] + [VMEM] * 6, out_specs=(VMEM, VMEM), compiler_params=PARAMS, name="conv_grads",
    )(own_support, upstream, signal, taps_high, taps_low, *tables(lags))
    result = result.reshape(seq_count, block_len, chan_count, share).transpose(0, 2, 1, 3).reshape(devices, part)
    mixed = jnp.concatenate([result, *split_outside(filter_grad.reshape(devices, own))], axis=1)
    mixed = lax.all_to_all(mixed, EVERY, split_axis=0, concat_axis=0, tiled=True)
    grad_inputs = mixed[:, :part].reshape(devices, block_len, share).transpose(1, 0, 2).reshape(block_len, width_here)
    filter_grad = mixed[:, part : part + own].astype(F32) + mixed[:, part + own :].astype(F32)
    filter_grad = filter_grad.reshape(devices, rows_each, chan_count, share).transpose(1, 2, 0, 3)
    return grad_inputs, filter_grad.reshape(filter_taps.shape)


def solution(mesh):
    seq_count, chan_count = mesh.shape["seq"], mesh.shape["chan"]

    def body(inputs, grads, filter_taps, supports):
        share = inputs.shape[1] // (seq_count * chan_count)
        lags = filter_taps.shape[0] * seq_count * chan_count
        fits = chan_count == 4 and share * 4 == LANES and filter_taps.shape[0] % 8 == 0
        fits = fits and inputs.shape[0] % 64 == 0 and lags % inputs.shape[0] == 0
        chosen = fast_body if fits else plain_body
        return chosen(inputs, grads, filter_taps, supports, seq_count, chan_count)

    in_specs = (P("seq", "chan"), P("seq", "chan"), P(("seq", "chan"), None), P())
    out_specs = (P("seq", "chan"), P(("seq", "chan"), None))
    return jax.shard_map(body, mesh=mesh, in_specs=in_specs, out_specs=out_specs, check_vma=False)
```

```python
import functools

import numpy as np
import ml_dtypes
import jax
import jax.numpy as jnp
from jax import lax
from jax.experimental import pallas as pl
from jax.experimental.pallas import tpu as pltpu
from jax.sharding import PartitionSpec as P

GROUP_CH = 128
LANES = 128
BF16 = jnp.bfloat16
F32 = jnp.float32
EVERY = ("seq", "chan")
VMEM = pl.BlockSpec(memory_space=pltpu.VMEM)
HBM = pl.BlockSpec(memory_space=pltpu.HBM)
SMEM = pl.BlockSpec(memory_space=pltpu.SMEM)
PARAMS = pltpu.CompilerParams(vmem_limit_bytes=40 * 1024 * 1024)


def split_table(table):
    high = table.astype(ml_dtypes.bfloat16)
    low = (table - high.astype(np.float64)).astype(ml_dtypes.bfloat16)
    return high, low


def tables(lags):
    freqs = np.concatenate([np.arange(0, lags, 2), np.arange(1, lags, 2)]) + 0.5
    angle = freqs[:, None] * np.arange(lags)[None, :] * (np.pi / lags)
    forward = np.concatenate([np.cos(angle), -np.sin(angle)], axis=0)
    high, low = split_table(forward)
    back_high, back_low = split_table(forward.T / lags)
    joined = (np.concatenate([high, low], axis=1), np.concatenate([back_high, back_high, back_low], axis=1))
    return [jnp.asarray(part) for part in joined]


def split_values(values):
    high = values.astype(BF16)
    return high, (values - high.astype(F32)).astype(BF16)


def split_outside(values):
    high = lax.reduce_precision(values, 8, 7)
    return [high.astype(BF16), (values - high).astype(BF16)]


def dot(first, second):
    return jnp.dot(first, second, preferred_element_type=F32)


def dot_exact(table, values):
    return dot(table, jnp.concatenate([values, values], axis=0))


def dot_split(table, values):
    high, low = split_values(values)
    return dot(table, jnp.concatenate([high, low, high], axis=0))


def conj_product(first, second, half):
    first_re, first_im = first[:half], first[half:]
    second_re, second_im = second[:half], second[half:]
    return jnp.concatenate(
        [first_re * second_re + first_im * second_im, first_im * second_re - first_re * second_im], axis=0
    )


def add_next(own, following, lags):
    quarter = lags // 2
    parts = [own[i * quarter : (i + 1) * quarter] for i in range(4)]
    nexts = [following[i * quarter : (i + 1) * quarter] for i in range(4)]
    return jnp.concatenate(
        [parts[0] + nexts[2], parts[1] - nexts[3], parts[2] - nexts[0], parts[3] + nexts[1]], axis=0
    )


def transform(dot_with, table, parts):
    width = parts[0].shape[1]
    group = 2 if width == LANES else 1
    found = []
    for i in range(0, len(parts), group):
        pair = parts[i : i + group]
        joined = dot_with(table, jnp.concatenate(pair, axis=1) if len(pair) > 1 else pair[0])
        found += [joined[:, k * width : (k + 1) * width] for k in range(len(pair))]
    return found


def conv_grads(lags, upstream, signal, taps, limit, forward, inverse):
    blocks = len(upstream)
    taps_high, taps_low = transform(dot_exact, forward, taps)
    taps_spec = taps_high + taps_low
    specs = transform(dot_exact, forward, upstream)
    results, filter_spec = [], None
    for start in range(0, blocks, 2):
        pair = range(start, min(start + 2, blocks))
        signal_specs = transform(dot_exact, forward, [signal[k] for k in pair])
        windows = [add_next(specs[k], specs[k + 1], lags) if k + 1 < blocks else specs[k] for k in pair]
        results += transform(dot_split, inverse, [conj_product(window, taps_spec, lags) for window in windows])
        for window, signal_spec in zip(windows, signal_specs):
            term = conj_product(window, signal_spec, lags)
            filter_spec = term if filter_spec is None else filter_spec + term
    (filter_grad,) = transform(dot_split, inverse, [filter_spec])
    lag_pos = lax.broadcasted_iota(jnp.int32, filter_grad.shape, 0)
    return results, jnp.where(lag_pos < limit, filter_grad, 0.0)


def swap_table():
    quarter = LANES // 4
    row = lax.broadcasted_iota(jnp.int32, (quarter, LANES), 0)
    lane = lax.broadcasted_iota(jnp.int32, (quarter, LANES), 1)
    zeros = jnp.zeros((quarter, LANES), BF16)
    slabs = []
    for part in range(4):
        pattern = jnp.where(lane == row + part * quarter, 1.0, 0.0).astype(BF16)
        slabs += [
            jnp.concatenate([pattern if at == block else zeros for at in range(4)], axis=1) for block in range(4)
        ]
    return jnp.concatenate(slabs, axis=0)


def swap_blocks(stacks, table):
    moved = dot(jnp.concatenate([jnp.concatenate(parts, axis=1) for parts in stacks], axis=0), table).astype(BF16)
    results, start = [], 0
    for parts in stacks:
        stop = start + parts[0].shape[0]
        results.append([moved[start:stop, l * LANES : (l + 1) * LANES] for l in range(4)])
        start = stop
    return results


def split_rows(values):
    high = values.astype(BF16).astype(F32)
    return jnp.concatenate([high, values - high], axis=0).astype(BF16)


def pack_kernel(grad_hbm, signal_hbm, taps_hbm, out_ref, grad_ref, signal_ref, taps_ref, sems):
    pairs = ((grad_hbm, grad_ref), (signal_hbm, signal_ref), (taps_hbm, taps_ref))
    arriving = [pltpu.make_async_copy(source, target, sems.at[i]) for i, (source, target) in enumerate(pairs)]
    for copy in arriving:
        copy.start()
    rows, width_here = grad_ref.shape
    piece = rows // 4
    tiles = range(width_here // LANES)

    table = swap_table()
    for copy in arriving:
        copy.wait()
    stacks = []
    for source in (grad_ref, signal_ref):
        for tile in tiles:
            columns = slice(tile * LANES, (tile + 1) * LANES)
            stacks.append([source[q * piece : (q + 1) * piece, columns] for q in range(4)])
    for tile in tiles:
        starts = [c * width_here + tile * LANES for c in range(4)]
        stacks.append([split_rows(taps_ref[:, start : start + LANES]) for start in starts])
    moved = swap_blocks(stacks, table)
    count = len(tiles)
    cuts = (slice(0, piece), slice(piece, 2 * piece), slice(2 * piece, out_ref.shape[1]))
    for index, cut in enumerate(cuts):
        for tile in tiles:
            for l in range(4):
                out_ref[tile * 4 + l, cut, :] = moved[index * count + tile][l]


def lane_limit(supports, width):
    lane = lax.broadcasted_iota(jnp.int32, (1, width), 1)
    limit = jnp.zeros((1, width), jnp.int32)
    for part, support in enumerate(supports):
        limit = jnp.where(lane >= part * (width // len(supports)), support * GROUP_CH, limit)
    return limit


def mask_taps(parts, limit):
    lag_pos = lax.broadcasted_iota(jnp.int32, parts[0].shape, 0)
    return [jnp.where(lag_pos < limit, part, 0.0).astype(BF16) for part in parts]


def fast_kernel(
    lags, piece, support_hbm, mixed_ref, forward_ref, inverse_ref, out_ref, support_ref, sem
):
    support_copy = pltpu.make_async_copy(support_hbm, support_ref, sem)
    support_copy.start()
    devices, rows, width = mixed_ref.shape
    seq_count = devices // 4
    own = (rows - 2 * piece) // 2
    per_block = lags // (4 * piece)
    table = swap_table()

    stacks = [
        [mixed_ref[s * 4 + c, at : at + piece, :] for c in range(4)] for at in (0, piece) for s in range(seq_count)
    ]
    flat = [part for parts in swap_blocks(stacks, table) for part in parts]
    size = 4 * per_block
    joined = [jnp.concatenate(flat[k : k + size], axis=0) for k in range(0, len(flat), size)]
    upstream, signal = joined[: len(joined) // 2], joined[len(joined) // 2 :]
    tap_parts = mixed_ref[:, 2 * piece :, :].astype(F32)
    groups_here = support_ref.shape[0] // 4
    index = lax.axis_index("seq")
    support_copy.wait()
    limit = lane_limit([support_ref[c * groups_here + index] for c in range(4)], width)
    taps = mask_taps([tap_parts[:, i * own : (i + 1) * own].reshape(lags, width) for i in range(2)], limit)
    results, filter_grad = conv_grads(lags, upstream, signal, taps, limit, forward_ref[...], inverse_ref[...])
    for j in range(devices):
        out_ref[j, piece:, :] = split_rows(filter_grad[j * own : (j + 1) * own])
    stacks = []
    for s in range(seq_count):
        result = results[s // per_block].astype(BF16)
        start = (s % per_block) * 4 * piece
        stacks.append([result[start + q * piece : start + (q + 1) * piece] for q in range(4)])
    moved = swap_blocks(stacks, table)
    for s in range(seq_count):
        for c in range(4):
            out_ref[s * 4 + c, 0:piece, :] = moved[s][c]


def unpack_kernel(mixed_ref, out_hbm, filter_hbm, out_ref, filter_ref, sems):
    rows, width_here = out_ref.shape
    piece = rows // 4
    own = filter_ref.shape[0]
    tiles = range(width_here // LANES)
    table = swap_table()
    cuts = (slice(0, piece), slice(piece, mixed_ref.shape[1]))
    moved = swap_blocks([[mixed_ref[tile * 4 + l, cut, :] for l in range(4)] for cut in cuts for tile in tiles], table)
    for tile in tiles:
        for q in range(4):
            out_ref[q * piece : (q + 1) * piece, tile * LANES : (tile + 1) * LANES] = moved[tile][q]
    first = pltpu.make_async_copy(out_ref, out_hbm, sems.at[0])
    first.start()
    for tile in tiles:
        for c in range(4):
            both = moved[len(tiles) + tile][c].astype(F32)
            start = c * width_here + tile * LANES
            filter_ref[:, start : start + LANES] = both[:own] + both[own:]
    second = pltpu.make_async_copy(filter_ref, filter_hbm, sems.at[1])
    second.start()
    first.wait()
    second.wait()


def fast_body(inputs, grads, filter_taps, supports, seq_count, chan_count):
    block_len, width_here = inputs.shape
    rows_each = filter_taps.shape[0]
    devices = seq_count * chan_count
    lags = rows_each * devices
    piece = block_len // 4
    sources = [pltpu.with_memory_space_constraint(part, pltpu.HBM) for part in (grads, inputs, filter_taps)]
    mixed = pl.pallas_call(
        pack_kernel,
        out_shape=pltpu.VMEM((devices, 2 * piece + 2 * rows_each, LANES), BF16),
        in_specs=[HBM] * 3, out_specs=VMEM,
        scratch_shapes=[
            pltpu.VMEM(inputs.shape, BF16), pltpu.VMEM(inputs.shape, BF16),
            pltpu.VMEM(filter_taps.shape, F32), pltpu.SemaphoreType.DMA((3,)),
        ],
        compiler_params=PARAMS, name="pack",
    )(*sources)
    mixed = lax.all_to_all(mixed, EVERY, split_axis=0, concat_axis=0, tiled=True)
    mixed = pl.pallas_call(
        functools.partial(fast_kernel, lags, piece),
        out_shape=jax.ShapeDtypeStruct((devices, piece + 2 * rows_each, LANES), BF16),
        in_specs=[HBM] + [VMEM] * 3, out_specs=VMEM,
        scratch_shapes=[pltpu.SMEM(supports.shape, jnp.int32), pltpu.SemaphoreType.DMA],
        compiler_params=PARAMS, name="conv_grads",
    )(pltpu.with_memory_space_constraint(supports, pltpu.HBM), mixed, *tables(lags))
    mixed = lax.all_to_all(mixed, EVERY, split_axis=0, concat_axis=0, tiled=True)
    return pl.pallas_call(
        unpack_kernel,
        out_shape=(
            jax.ShapeDtypeStruct((block_len, width_here), BF16),
            jax.ShapeDtypeStruct(filter_taps.shape, F32),
        ),
        in_specs=[VMEM], out_specs=(HBM, HBM),
        scratch_shapes=[
            pltpu.VMEM((block_len, width_here), BF16), pltpu.VMEM(filter_taps.shape, F32),
            pltpu.SemaphoreType.DMA((2,)),
        ],
        compiler_params=PARAMS, name="unpack",
    )(mixed)


def plain_kernel(
    lags, support_ref, grad_ref, signal_ref, high_ref, low_ref, forward_ref, inverse_ref, out_ref, filter_ref
):
    total, width = grad_ref.shape
    limit = lane_limit([support_ref[part] for part in range(support_ref.shape[0])], width)
    taps = mask_taps([high_ref[...].astype(F32), low_ref[...].astype(F32)], limit)
    cuts = [slice(k * lags, (k + 1) * lags) for k in range(total // lags)]
    results, filter_grad = conv_grads(
        lags, [grad_ref[cut, :] for cut in cuts], [signal_ref[cut, :] for cut in cuts], taps, limit,
        forward_ref[...], inverse_ref[...],
    )
    for cut, result in zip(cuts, results):
        out_ref[cut, :] = result.astype(BF16)
    filter_ref[...] = filter_grad


def plain_body(inputs, grads, filter_taps, supports, seq_count, chan_count):
    block_len, width_here = inputs.shape
    rows_each = filter_taps.shape[0]
    devices = seq_count * chan_count
    lags = rows_each * devices
    total = block_len * seq_count
    share = width_here // devices
    width = share * chan_count
    index = lax.axis_index("seq") * chan_count + lax.axis_index("chan")
    groups_here = width_here // GROUP_CH
    own_support = lax.dynamic_slice_in_dim(
        supports.reshape(chan_count, groups_here), index * share // GROUP_CH, 1, 1
    ).reshape(chan_count)

    def sent(values):
        return values.reshape(block_len, devices, share).transpose(1, 0, 2).reshape(devices, -1)

    def received(values):
        return values.reshape(seq_count, chan_count, block_len, share).transpose(0, 2, 1, 3).reshape(total, width)

    taps = filter_taps.reshape(rows_each, chan_count, devices, share).transpose(2, 0, 1, 3).reshape(devices, -1)
    mixed = jnp.concatenate([sent(grads), sent(inputs), *split_outside(taps)], axis=1)
    mixed = lax.all_to_all(mixed, EVERY, split_axis=0, concat_axis=0, tiled=True)
    part, own = block_len * share, rows_each * width
    upstream, signal = received(mixed[:, :part]), received(mixed[:, part : 2 * part])
    taps_high = mixed[:, 2 * part : 2 * part + own].reshape(lags, width)
    taps_low = mixed[:, 2 * part + own :].reshape(lags, width)
    result, filter_grad = pl.pallas_call(
        functools.partial(plain_kernel, lags),
        out_shape=(jax.ShapeDtypeStruct((total, width), BF16), jax.ShapeDtypeStruct((lags, width), F32)),
        in_specs=[SMEM] + [VMEM] * 6, out_specs=(VMEM, VMEM), compiler_params=PARAMS, name="conv_grads",
    )(own_support, upstream, signal, taps_high, taps_low, *tables(lags))
    result = result.reshape(seq_count, block_len, chan_count, share).transpose(0, 2, 1, 3).reshape(devices, part)
    mixed = jnp.concatenate([result, *split_outside(filter_grad.reshape(devices, own))], axis=1)
    mixed = lax.all_to_all(mixed, EVERY, split_axis=0, concat_axis=0, tiled=True)
    grad_inputs = mixed[:, :part].reshape(devices, block_len, share).transpose(1, 0, 2).reshape(block_len, width_here)
    filter_grad = mixed[:, part : part + own].astype(F32) + mixed[:, part + own :].astype(F32)
    filter_grad = filter_grad.reshape(devices, rows_each, chan_count, share).transpose(1, 2, 0, 3)
    return grad_inputs, filter_grad.reshape(filter_taps.shape)


def solution(mesh):
    seq_count, chan_count = mesh.shape["seq"], mesh.shape["chan"]

    def body(inputs, grads, filter_taps, supports):
        share = inputs.shape[1] // (seq_count * chan_count)
        lags = filter_taps.shape[0] * seq_count * chan_count
        fits = chan_count == 4 and share * 4 == LANES and filter_taps.shape[0] % 8 == 0
        fits = fits and inputs.shape[0] % 64 == 0 and lags % inputs.shape[0] == 0
        chosen = fast_body if fits else plain_body
        return chosen(inputs, grads, filter_taps, supports, seq_count, chan_count)

    in_specs = (P("seq", "chan"), P("seq", "chan"), P(("seq", "chan"), None), P())
    out_specs = (P("seq", "chan"), P(("seq", "chan"), None))
    return jax.shard_map(body, mesh=mesh, in_specs=in_specs, out_specs=out_specs, check_vma=False)
```
